256 devices in a mesh: row: 8 (over y, core), col: 32 (over x, z).
Axes of the slice: x: 4, y: 4, z: 8, core: 2. Of those that a mesh axis runs over, the one named last changes fastest.
Arguments:
- positions: float32 [32, 3, 8192], P(None, None, ('row', 'col')), may hold values from -1 to 64, as said below
- charges: float32 [8192], P(('row', 'col')), may hold values from -3 to 3
- atom_types: int32 [8192], P(('row', 'col')), may hold values from 0 to 31
- exclusions: int32 [8192], P('row'), may hold values from 0 to 1073741823, as said below
- type_radius: float32 [32], replicated, may hold values from 1.1 to 2
- type_volume: float32 [32], replicated, may hold values from 0.03 to 0.3
Outputs:
- forces: float32 [32, 3, 8192], P(None, None, ('row', 'col'))
- born_radii: float32 [32, 8192], P(None, ('row', 'col'))
The draws below stay inside these ranges and needn't reach their ends.
Inputs may be any that keep to these rules, and one draw needn't show every extreme that they name: `positions`: within one conformation no two atoms are closer than 0.8. Bit k (k < 15) of exclusions[a] marks the pair a, a + k + 1 and bit 15 + k marks the pair a, a - k - 1; the two marks of one pair agree, and no bit names an atom outside 0 to 8191.
All inputs are finite; a program needn't handle non-finite values.
Results may differ from the reference program's by a relative error of at most 0.0003.
Values sent between devices are 32-bit elements; how exact they have to be, the bound alone decides.
A program may use at most 64 MiB of HBM per device.

```python
import math
from functools import partial
import jax
import jax.numpy as jnp
from jax import lax

REPLICAS = 32
NTYPES = 32
ATOMS = 8192


def draw_positions(key, part):
    key = jax.random.fold_in(key, 11)
    order_key, jitter_key = jax.random.split(key)
    atom_index = jnp.arange(ATOMS, dtype=jnp.int32)
    placement = jax.random.permutation(order_key, ATOMS // 16).astype(jnp.int32)
    brick = placement[atom_index // 16]
    within = atom_index % 16
    lattice = jnp.stack([within % 4 + 4 * (brick % 4), within // 4 + 4 * (brick // 4 % 4), brick // 16]).astype(jnp.float32) * 1.6
    jitter = 0.4 * jnp.tanh(jax.random.normal(jitter_key, (REPLICAS, 3, ATOMS), jnp.float32))
    return lattice[None] + jitter


def draw_exclusions(key, part):
    key = jax.random.fold_in(key, 23)
    atom_index = jnp.arange(ATOMS, dtype=jnp.int32)
    forward = jax.random.randint(key, (ATOMS,), 0, 32768, dtype=jnp.int32)
    centre = ATOMS // 2
    forward = jnp.where((atom_index >= centre - 15) & (atom_index <= centre), 32767, forward)
    headroom = jnp.clip(ATOMS - 1 - atom_index, 0, 15).astype(jnp.int32)
    forward = jnp.bitwise_and(forward, jnp.left_shift(jnp.ones((ATOMS,), jnp.int32), headroom) - 1)
    backward = jnp.zeros((ATOMS,), jnp.int32)
    for offset in range(15):
        earlier = jnp.concatenate([jnp.zeros((offset + 1,), jnp.int32), forward[:ATOMS - offset - 1]])
        bitflag = jnp.bitwise_and(jnp.right_shift(earlier, offset), 1)
        backward = jnp.bitwise_or(backward, jnp.left_shift(bitflag, 15 + offset))
    return jnp.bitwise_or(forward, backward)


def set_ends(values, stream_key, low, top_value):
    longest = values.shape.index(max(values.shape))
    spots = []
    for shift in (0, 1):
        where = [jax.random.randint(jax.random.fold_in(stream_key, axis), (), 0, length) for axis, length in enumerate(values.shape)]
        where[longest] = (where[longest] + shift) % values.shape[longest]
        spots.append(tuple(where))
    return values.at[spots[0]].set(low).at[spots[1]].set(top_value)


def block_levels(own_key, extent, cuts, low, high):
    gain = 1.0
    for position, blocks in cuts:
        draws = jax.random.uniform(jax.random.fold_in(jax.random.fold_in(own_key, 6), position), (blocks,), jnp.float32, low / len(cuts), high / len(cuts))
        gain = gain * jnp.repeat(jnp.exp(draws), extent[position] // blocks).reshape((-1,) + (1,) * (len(extent) - 1 - position))
    return gain


def bell_draw(own_key, shape, spread, limit, cuts=(), held_as=jnp.bfloat16):
    drawn = spread * jax.random.normal(own_key, shape, jnp.float32)
    if cuts:
        drawn = drawn * block_levels(own_key, shape, cuts, -0.22, 0.18)
    return jnp.clip(drawn, -limit, limit).astype(held_as)


def setup_inputs(seed: int = 0) -> dict:
    arg_keys = jax.random.split(jax.random.key(seed), 7)
    positions = draw_positions(jax.random.fold_in(arg_keys[6], 71), 0)
    charges = bell_draw(arg_keys[1], (ATOMS,), 0.5, 3.0, ((0, 256),), jnp.float32)
    atom_types = set_ends(jax.random.randint(arg_keys[2], (ATOMS,), 0, NTYPES), jax.random.fold_in(arg_keys[2], 1), 0, NTYPES - 1).astype(jnp.int32)
    exclusions = draw_exclusions(jax.random.fold_in(arg_keys[6], 71), 0)
    type_radius = jnp.clip(jnp.exp(jax.random.uniform(arg_keys[4], (NTYPES,), jnp.float32, math.log(1.1), math.log(2.0))), 1.1, 2.0)
    type_volume = jnp.clip(jnp.exp(jax.random.uniform(arg_keys[5], (NTYPES,), jnp.float32, math.log(0.03), math.log(0.3))), 0.03, 0.3)
    return dict(positions=positions, charges=charges, atom_types=atom_types, exclusions=exclusions, type_radius=type_radius, type_volume=type_volume)


SOLVENT_FACTOR = 1.0 - 1.0 / 78.5

def geometry(rowrep, colrep):
    displace = rowrep[0:3, :, :, None] - colrep[0:3, :, None, :]
    distsq = lax.optimization_barrier(jnp.sum(displace * displace, axis=0))
    return (displace, distsq)

def pair_masks(row_ids, col_ids, row_masks):
    shift_gap = col_ids[None, :] - row_ids[:, None]
    paired = shift_gap != 0
    nearby = paired & (jnp.abs(shift_gap) <= 15)
    bitpos = jnp.where(shift_gap > 0, shift_gap - 1, 14 - shift_gap)
    bitpos = jnp.where(nearby, bitpos, 0).astype(jnp.int32)
    bitflag = jnp.bitwise_and(jnp.right_shift(row_masks[:, None], bitpos), 1)
    excluded = nearby & (bitflag == 1)
    weight = jnp.where(paired & jnp.logical_not(excluded), 1.0, 0.0).astype(jnp.float32)
    return (weight, paired)

def coulomb_grad(displace, distsq, rowatom, colatom, weight, paired):
    guarded = jnp.where(paired[None], distsq, 1.0)
    inverse = lax.rsqrt(guarded)
    factor = -(weight * rowatom[0][:, None] * colatom[0][None, :])[None] * inverse * inverse * inverse
    return lax.optimization_barrier(jnp.sum(factor[None] * displace, axis=3))

def descreen_kernel(rowrep, colrep, rowatom, colatom, row_ids, col_ids, row_masks, coul_first):
    displace, distsq = geometry(rowrep, colrep)
    weight, paired = pair_masks(row_ids, col_ids, row_masks)
    denom = distsq + (colatom[2] * colatom[2])[None, None, :]
    inverse = 1.0 / denom
    descreen = jnp.where(paired[None], colatom[1][None, None, :] * inverse * inverse, 0.0)
    pieces = [lax.optimization_barrier(jnp.sum(descreen, axis=2))[None]]
    if coul_first:
        pieces.append(coulomb_grad(displace, distsq, rowatom, colatom, weight, paired))
    return jnp.concatenate(pieces, axis=0)

def born_kernel(rowrep, colrep, rowatom, colatom, row_ids, col_ids, row_masks, coul_last):
    displace, distsq = geometry(rowrep, colrep)
    radius_row = rowrep[3][:, :, None]
    radius_col = colrep[3][:, None, :]
    product = radius_row * radius_col
    damping = jnp.exp(-distsq / (4.0 * product))
    effective = distsq + product * damping
    reciprocal = lax.rsqrt(effective)
    cubed = reciprocal * reciprocal * reciprocal
    charge_pair = SOLVENT_FACTOR * (rowatom[0][:, None] * colatom[0][None, :])[None]
    direct = lax.optimization_barrier(jnp.sum((charge_pair * cubed * (1.0 - 0.25 * damping))[None] * displace, axis=3))
    radial = lax.optimization_barrier(jnp.sum(0.5 * charge_pair * cubed * damping * (1.0 + distsq / (4.0 * product)) * radius_col, axis=2))
    pieces = [radial[None], direct]
    if coul_last:
        weight, paired = pair_masks(row_ids, col_ids, row_masks)
        pieces.append(coulomb_grad(displace, distsq, rowatom, colatom, weight, paired))
    return jnp.concatenate(pieces, axis=0)

def chain_kernel(rowrep, colrep, rowatom, colatom, row_ids, col_ids, row_masks):
    displace, distsq = geometry(rowrep, colrep)
    weight, paired = pair_masks(row_ids, col_ids, row_masks)
    inv_row = 1.0 / (distsq + (rowatom[2] * rowatom[2])[None, :, None])
    inv_col = 1.0 / (distsq + (colatom[2] * colatom[2])[None, None, :])
    factor = rowrep[3][:, :, None] * colatom[1][None, None, :] * inv_col * inv_col * inv_col
    factor = factor + colrep[3][:, None, :] * rowatom[1][None, :, None] * inv_row * inv_row * inv_row
    factor = jnp.where(paired[None], -4.0 * factor, 0.0)
    return lax.optimization_barrier(jnp.sum(factor[None] * displace, axis=3))

def radii(radius, integral):
    saturation = jnp.tanh(radius * integral)
    born = 1.0 / (1.0 / radius - saturation / (radius + 0.09))
    slope = born * born * (1.0 - saturation * saturation) * radius / (radius + 0.09)
    return (born, slope)

def run_pass(kernel, rowrep, colrep, rowatom, colatom, row_ids, col_ids, row_masks, fields):
    planes, replicas, row_len = rowrep.shape
    col_len = colrep.shape[2]
    group = math.gcd(replicas, 8)
    groups = replicas // group
    tile_len = 128 if col_len % 128 == 0 else col_len
    tiles = col_len // tile_len
    row_groups = rowrep.reshape(planes, groups, group, row_len).transpose(1, 0, 2, 3)
    col_groups = colrep.reshape(planes, groups, group, tiles, tile_len).transpose(1, 3, 0, 2, 4)
    col_atoms = colatom.reshape(colatom.shape[0], tiles, tile_len).transpose(1, 0, 2)
    col_tiles = col_ids.reshape(tiles, tile_len)

    def one_group(inputs):
        row_block, col_block = inputs

        def advance(running, pieces):
            col_tile, atom_tile, id_tile = pieces
            return (running + kernel(row_block, col_tile, rowatom, atom_tile, row_ids, id_tile, row_masks), None)
        start = jnp.zeros((fields, group, row_len), jnp.float32)
        running, _ = lax.scan(advance, start, (col_block, col_atoms, col_tiles))
        return running
    result = lax.map(one_group, (row_groups, col_groups))
    return result.transpose(1, 0, 2, 3).reshape(fields, replicas, row_len)

def reference(positions, charges, atom_types, exclusions, type_radius, type_volume):
    count = positions.shape[2]
    radius = type_radius[atom_types]
    volume = type_volume[atom_types]
    atoms = jnp.stack([charges, volume, radius])
    layout = positions.transpose(1, 0, 2)
    atom_ids = jnp.arange(count, dtype=jnp.int32)
    first = run_pass(partial(descreen_kernel, coul_first=False), layout, layout, atoms, atoms, atom_ids, atom_ids, exclusions, 1)
    born, slope = radii(radius[None, :], first[0])
    with_born = jnp.concatenate([layout, born[None]], axis=0)
    second = run_pass(partial(born_kernel, coul_last=True), with_born, with_born, atoms, atoms, atom_ids, atom_ids, exclusions, 7)
    chained = second[0] * slope
    with_chain = jnp.concatenate([layout, chained[None]], axis=0)
    third = run_pass(chain_kernel, with_chain, with_chain, atoms, atoms, atom_ids, atom_ids, exclusions, 3)
    gradient = second[1:4] + second[4:7] + third
    return ((-gradient).transpose(1, 0, 2), born)
```

```python
import functools
import math

import jax
import jax.numpy as jnp
from jax import lax
from jax.experimental import pallas as pl
from jax.experimental.pallas import tpu as pltpu
from jax.sharding import PartitionSpec as P

F32 = jnp.float32
BF16 = jnp.bfloat16
MESH = pl.DeviceIdType.MESH
TAU = 1.0 - 1.0 / 78.5
SIGMA = math.log2(math.e)
CENTRE = 32.0

ROWS = 8
COLS = 32
OWN = 1024
ATOMS = ROWS * OWN
HALF = 5 * OWN
STRIP = 256
CHUNK1 = 512
CHUNK2 = 512


def narrow(value):
    return value.astype(BF16).astype(F32)


def split3(value):
    first = narrow(value)
    second = narrow(value - first)
    return first, second, value - first - second


def row_index(shape):
    return lax.broadcasted_iota(jnp.int32, shape, 0)


def three_rows(value, at):
    pieces = split3(value)
    row = row_index((8, value.shape[1]))
    out = jnp.zeros((8, value.shape[1]), F32)
    for k, piece in enumerate(pieces):
        out = jnp.where(row == at + k, piece, out)
    return out


def features(block, left):
    n = block.shape[1]
    row = row_index((8, n))
    x = jnp.where(row < 3, block, 0.0)
    coarse = jnp.floor(x * 16.0 + 0.5) * 0.0625
    fine = x - coarse
    ch = narrow(coarse)
    cl = coarse - ch
    f1 = narrow(fine)
    f2 = narrow(fine - f1)
    norm = jnp.sum(coarse * coarse, axis=0, keepdims=True)
    rest = jnp.sum((2.0 * coarse + fine) * fine, axis=0, keepdims=True)
    ones_lo = jnp.where(row < 3, 1.0, 0.0)
    ones_mid = jnp.where((row >= 3) & (row < 6), 1.0, 0.0)
    if left:
        ch2, cl2, f12, f22 = (-2.0 * v for v in (ch, cl, f1, f2))
        groups = [ch2, ch2, cl2, cl2, three_rows(norm, 0) + ones_mid]
        groups += [ch2, ch2, cl2, cl2, f12, f12, f22, f22]
        groups += [f12 + three_rows(rest, 3), f12 + ones_mid, f22 + ones_mid]
    else:
        radius = block[4:5]
        groups = [ch, cl, ch, cl, ones_lo + three_rows(norm, 3)]
        groups += [f1, f2, f1, f2, ch, cl, ch, cl]
        groups += [f1 + ones_mid, f2 + three_rows(rest, 3), f1 + three_rows(radius * radius, 3)]
    return jnp.concatenate(groups, axis=0)


def weights(placed, scale):
    first, second, third = split3(placed * scale)
    return jnp.concatenate([first + pltpu.roll(second, 4, 0), third], axis=0).astype(BF16)


def gather_pieces(sums):
    top = sums[0:8]
    return top + pltpu.roll(top, 4, 0) + sums[8:16]


def spread(row, out_ref):
    for k in range(OWN // 128):
        piece = jnp.broadcast_to(row[:, k * 128 : (k + 1) * 128], (128, 128))
        out_ref[k * 128 : (k + 1) * 128, :] = jnp.transpose(piece)


def lane_sums(value):
    out = lax.dot_general(
        jnp.ones((8, 128), F32),
        value,
        (((1,), (1,)), ((), ())),
        precision=lax.Precision.HIGHEST,
        preferred_element_type=F32,
    )
    return out[0:1]


def kernel(
    send_ref, excl_ref, out_ref,
    inbox, atoms, placed, right, left, left2, cubes, weight, integral,
    born_all, damp_all, charge_row, damp_col, qborn_col, excl_col, rad_rows, rad_cols, side_cols,
    own_force, rad_send, rad_recv, force_send, force_recv, result,
    in_s, in_r, at_s, at_r, bn_s, bn_r, rd_s, rd_r, fc_s, fc_r, out_s, out_r,
):
    r = lax.axis_index("row")
    c = lax.axis_index("col")

    def col_peer(d):
        return (r, lax.rem(c + d, COLS))

    def row_peer(d):
        return (lax.rem(r + d + ROWS, ROWS), c)

    barrier = pltpu.get_barrier_semaphore()

    @pl.loop(1, COLS)
    def _(d):
        pl.semaphore_signal(barrier, inc=1, device_id=col_peer(d), device_id_type=MESH)

    @pl.loop(1, ROWS)
    def _(d):
        pl.semaphore_signal(barrier, inc=1, device_id=row_peer(d), device_id_type=MESH)

    pl.semaphore_wait(barrier, COLS - 1 + ROWS - 1)

    def in_copy(d):
        peer = col_peer(d)
        return pltpu.make_async_remote_copy(
            src_ref=send_ref.at[peer[1]], dst_ref=inbox.at[c],
            send_sem=in_s.at[d], recv_sem=in_r.at[d], device_id=peer, device_id_type=MESH,
        )

    @pl.loop(1, COLS)
    def _(d):
        in_copy(d).start()

    inbox[c] = send_ref[c]
    spread(excl_ref[...], excl_col)

    @pl.loop(1, COLS)
    def _(d):
        in_copy(d).wait_recv()

    for g in range(OWN // 128):
        atoms[:, g * 128 : (g + 1) * 128] = (
            (inbox[4 * g] + inbox[4 * g + 1]) + (inbox[4 * g + 2] + inbox[4 * g + 3])
        )

    def atom_copy(j):
        start = pl.multiple_of(j * OWN, OWN)
        return pltpu.make_async_remote_copy(
            src_ref=atoms.at[:, pl.ds(0, OWN)], dst_ref=atoms.at[:, pl.ds(start, OWN)],
            send_sem=at_s.at[j], recv_sem=at_r.at[j], device_id=row_peer(-j), device_id_type=MESH,
        )

    for j in range(1, ROWS):
        atom_copy(j).start()

    whole = features(atoms[:, 0:OWN], True)
    for k in range(OWN // 128):
        piece = jnp.transpose(whole[:, k * 128 : (k + 1) * 128])
        left[k * 128 : (k + 1) * 128, :] = piece.astype(BF16)
        lane = lax.broadcasted_iota(jnp.int32, (128, 128), 1)
        piece = jnp.where((lane >= 123) & (lane < 126), 0.0, piece)
        left2[k * 128 : (k + 1) * 128, :] = piece.astype(BF16)

    integral[...] = jnp.zeros_like(integral)

    def first_pass(j):
        base = pl.multiple_of(j * OWN, OWN)
        block = atoms[:, pl.ds(base, OWN)]
        right[:, pl.ds(base, OWN)] = features(block, False).astype(BF16)
        row = row_index((8, OWN))
        here = jnp.where(row < 3, block - CENTRE, jnp.where(row == 3, 1.0, 0.0))
        placed[:, pl.ds(base, OWN)] = here
        weight[:, pl.ds(base, OWN)] = weights(here, block[5:6])

        for t in range(OWN // CHUNK1):
            c0 = pl.multiple_of(base + t * CHUNK1, CHUNK1)
            cols = right[:, pl.ds(c0, CHUNK1)]
            volume = atoms[5:6, pl.ds(c0, CHUNK1)]

            @pl.loop(0, OWN // STRIP)
            def _(s):
                r0 = pl.multiple_of(s * STRIP, STRIP)
                denom = jnp.dot(left[pl.ds(r0, STRIP), :], cols, preferred_element_type=F32)
                inverse = pl.reciprocal(denom, approx=True)
                square = inverse * inverse
                term = square * volume
                total = integral[pl.ds(r0, STRIP), :]
                for q in range(CHUNK1 // 128):
                    total = total + term[:, q * 128 : (q + 1) * 128]
                integral[pl.ds(r0, STRIP), :] = total
                cubes[pl.ds(r0, STRIP), pl.ds(c0, CHUNK1)] = (square * inverse).astype(BF16)

    first_pass(0)

    @pl.loop(1, ROWS)
    def _(j):
        atom_copy(j).wait_recv()
        first_pass(j)

    charge = atoms[3:4, 0:OWN]
    radius = atoms[4:5, 0:OWN]
    volume = atoms[5:6, 0:OWN]
    own_inverse = 1.0 / (radius * radius)
    summed = lane_sums(integral[...]) - volume * own_inverse * own_inverse
    filled = jnp.tanh(radius * summed)
    born = 1.0 / (1.0 / radius - filled / (radius + 0.09))
    slope = born * born * (1.0 - filled * filled) * radius / (radius + 0.09)
    born_all[:, 0:OWN] = born

    def born_copy(j):
        return pltpu.make_async_remote_copy(
            src_ref=born_all.at[:, pl.ds(0, OWN)],
            dst_ref=born_all.at[:, pl.ds(pl.multiple_of(j * OWN, OWN), OWN)],
            send_sem=bn_s.at[j], recv_sem=bn_r.at[j], device_id=row_peer(-j), device_id_type=MESH,
        )

    for j in range(1, 5):
        born_copy(j).start()

    def own_descreen(j, sums):
        c0 = pl.multiple_of(j * OWN, OWN)
        return sums + lax.dot_general(
            weight[:, pl.ds(c0, OWN)], cubes[:, pl.ds(c0, OWN)],
            (((1,), (1,)), ((), ())), preferred_element_type=F32,
        )

    own_sums = lax.fori_loop(0, ROWS, own_descreen, jnp.zeros((16, OWN), F32))

    for j in range(1, 5):
        born_copy(j).wait_recv()

    radii = born_all[...]
    inverse_radii = 1.0 / radii
    damp = inverse_radii * (math.sqrt(SIGMA) * 0.5)
    damp_all[...] = damp
    lead = atoms[3:4, 0:HALF] * inverse_radii * lax.rsqrt(radii) * ((SIGMA * 0.25) ** 0.75)
    charge_row[...] = lead * radii
    weight[:, 0:HALF] = weights(placed[:, 0:HALF], lead)
    spread(damp[:, 0:OWN], damp_col)
    spread((lead * radii)[:, 0:OWN], qborn_col)
    rad_rows[...] = jnp.zeros_like(rad_rows)
    rad_cols[...] = jnp.zeros_like(rad_cols)
    side_cols[...] = jnp.zeros_like(side_cols)

    def pair_tile(r0, rows, c0, cols, special, both):
        distsq = jnp.dot(
            left2[pl.ds(r0, rows), :], right[:, pl.ds(c0, cols)], preferred_element_type=F32
        )
        row_damp = damp_col[pl.ds(r0, rows), :]
        row_charge = qborn_col[pl.ds(r0, rows), :]
        highs, lows = [], []
        rad = rad_rows[pl.ds(r0, rows), :]
        for q in range(cols // 128):
            here = pl.ds(pl.multiple_of(c0 + q * 128, 128), 128)
            y = distsq[:, q * 128 : (q + 1) * 128] * (row_damp * damp_all[:, here])
            masked = special and q * 128 < rows + 15
            if masked:
                gap = (
                    lax.broadcasted_iota(jnp.int32, (rows, 128), 1)
                    - lax.broadcasted_iota(jnp.int32, (rows, 128), 0)
                    + q * 128
                )
                near = jnp.abs(gap) <= 15
                bit = jnp.where(gap > 0, gap - 1, 14 - gap)
                bit = jnp.where(near & (gap != 0), bit, 0)
                marked = jnp.bitwise_and(jnp.right_shift(excl_col[pl.ds(r0, rows), :], bit), 1) == 1
                drop = (near & marked) | (gap == 0)
                y = jnp.where(gap == 0, 0.0, y)
            e = jnp.exp2(math.log2(SIGMA * 0.25) - y)
            g = lax.rsqrt(y + e)
            g3 = g * g * g
            i = lax.rsqrt(y)
            i3 = i * i * i
            if masked:
                i3 = jnp.where(drop, 0.0, i3)
            h = g3 * e
            force = (i3 - TAU * g3) + (TAU / SIGMA) * h
            radial = h * (SIGMA + y)
            high = force.astype(BF16)
            highs.append(high)
            lows.append((force - high.astype(F32)).astype(BF16))
            rad = rad + radial * charge_row[:, here]
            if q * 128 >= both:
                part = radial * row_charge
                total = part[0:8]
                for k in range(1, rows // 8):
                    total = total + part[k * 8 : (k + 1) * 8]
                rad_cols[:, here] += total
        rad_rows[pl.ds(r0, rows), :] = rad
        high = jnp.concatenate(highs, axis=1)
        low = jnp.concatenate(lows, axis=1)
        over = (((1,), (1,)), ((), ()))
        there = weight[:, pl.ds(c0, cols)]
        own_force[:, pl.ds(r0, rows)] += lax.dot_general(
            there, high, over, preferred_element_type=F32
        ) + lax.dot_general(there, low, over, preferred_element_type=F32)
        if both < cols:
            mine = weight[:, pl.ds(r0, rows)]
            kept = pl.ds(pl.multiple_of(c0 + both, 128), cols - both)
            side_cols[:, kept] += jnp.dot(
                mine, high[:, both:], preferred_element_type=F32
            ) + jnp.dot(mine, low[:, both:], preferred_element_type=F32)

    own_force[...] = jnp.zeros_like(own_force)
    swap = jnp.where(r >= ROWS // 2, 128, 0)

    @pl.loop(0, OWN // STRIP)
    def _(s):
        r0 = pl.multiple_of(s * STRIP, STRIP)
        pair_tile(r0, STRIP, r0, 2 * STRIP, True, STRIP)

        @pl.loop(0, 7)
        def _(t):
            c0 = pl.multiple_of(r0 + 2 * STRIP + t * CHUNK2, STRIP)
            pair_tile(r0, STRIP, c0, CHUNK2, False, 0)

        far = r0 + 16 * STRIP
        pair_tile(r0, 128, pl.multiple_of(far + swap, 128), 128, False, 0)
        pair_tile(
            pl.multiple_of(r0 + 128, 128), 128, pl.multiple_of(far + 128 - swap, 128), 128, False, 0
        )

    rad_send[...] = jnp.sum(rad_cols[...], axis=0, keepdims=True)

    def rad_copy(j):
        return pltpu.make_async_remote_copy(
            src_ref=rad_send.at[:, pl.ds(j * OWN, OWN)],
            dst_ref=rad_recv.at[:, pl.ds((j - 1) * OWN, OWN)],
            send_sem=rd_s.at[j], recv_sem=rd_r.at[j], device_id=row_peer(j), device_id_type=MESH,
        )

    for j in range(1, 5):
        rad_copy(j).start()
    radial = lane_sums(rad_rows[...]) + rad_send[:, 0:OWN]
    for j in range(1, 5):
        rad_copy(j).wait_recv()
    for j in range(4):
        radial = radial + rad_recv[:, j * OWN : (j + 1) * OWN]
    lead_own = charge * lax.rsqrt(born) / born * ((SIGMA * 0.25) ** 0.75)
    radial = radial * lead_own * (0.5 * TAU * 4.0 / (SIGMA * SIGMA))
    chained = radial * slope
    chain_weight = weights(placed[:, 0:OWN], chained)

    def last_block(j, direct):
        c0 = pl.multiple_of(j * OWN, OWN)
        here = pl.ds(c0, OWN)
        sums = gather_pieces(jnp.dot(chain_weight, cubes[:, here], preferred_element_type=F32))
        where_b = placed[:, here]
        force = (where_b * sums[3:4] - sums) * (4.0 * atoms[5:6, here])
        if direct:
            side = gather_pieces(side_cols[:, here])
            damp_b = damp_all[:, here] * (2.0 / math.sqrt(SIGMA))
            lead_b = atoms[3:4, here] * damp_b * jnp.sqrt(damp_b) * ((SIGMA * 0.25) ** 0.75)
            force = force + (where_b * side[3:4] - side) * lead_b
        force_send[:, here] = force[0:4]

    def force_copy(j):
        here = pl.ds(pl.multiple_of(j * OWN, OWN), OWN)
        return pltpu.make_async_remote_copy(
            src_ref=force_send.at[:, here], dst_ref=force_recv.at[:, here],
            send_sem=fc_s.at[j], recv_sem=fc_r.at[j], device_id=row_peer(j), device_id_type=MESH,
        )

    @pl.loop(1, 5)
    def _(j):
        last_block(j, True)
        force_copy(j).start()

    @pl.loop(5, ROWS)
    def _(j):
        last_block(j, False)
        force_copy(j).start()

    last_block(0, True)
    mine = placed[:, 0:OWN]
    sums = gather_pieces(own_sums)
    total = (mine * sums[3:4] - sums) * (4.0 * chained)
    sums = gather_pieces(own_force[...])
    total = total + (mine * sums[3:4] - sums) * lead_own
    total = total[0:4] + force_send[:, 0:OWN]

    for j in range(1, ROWS):
        force_copy(j).wait_recv()
    for j in range(1, ROWS):
        total = total + force_recv[:, j * OWN : (j + 1) * OWN]
    total = jnp.where(row_index((4, OWN)) == 3, born, total)
    for g in range(OWN // 128):
        result[g] = total[:, g * 128 : (g + 1) * 128]

    def out_copy(d):
        peer = col_peer(d)
        return pltpu.make_async_remote_copy(
            src_ref=result.at[peer[1] // 4], dst_ref=out_ref.at[c],
            send_sem=out_s.at[d], recv_sem=out_r.at[d], device_id=peer, device_id_type=MESH,
        )

    @pl.loop(1, COLS)
    def _(d):
        out_copy(d).start()

    out_ref[c] = result[c // 4]

    @pl.loop(1, COLS)
    def _(d):
        out_copy(d).wait()
        in_copy(d).wait_send()

    for j in range(1, 5):
        born_copy(j).wait_send()
        rad_copy(j).wait_send()
    for j in range(1, ROWS):
        atom_copy(j).wait_send()
        force_copy(j).wait_send()


def on_device(positions, charges, atom_types, exclusions, type_radius, type_volume):
    c = lax.axis_index("col")
    type_ids = jnp.arange(type_radius.shape[0], dtype=jnp.int32)
    onehot = (atom_types[:, None] == type_ids[None, :]).astype(F32)
    radius = jnp.sum(onehot * type_radius[None, :], axis=1)
    volume = jnp.sum(onehot * type_volume[None, :], axis=1)
    shared = jnp.stack([charges, radius, volume, jnp.zeros_like(volume), jnp.zeros_like(volume)])
    shared = jnp.broadcast_to(shared[None], (COLS, 5, 32))
    packed = jnp.concatenate([positions, shared], axis=1)
    lane = jnp.arange(128, dtype=jnp.int32) // 32
    packed = jnp.where(lane[None, None] == c % 4, jnp.tile(packed, (1, 1, 4)), 0.0)
    vmem = pl.BlockSpec(memory_space=pltpu.VMEM)
    dma = pltpu.SemaphoreType.DMA
    result = pl.pallas_call(
        kernel,
        out_shape=jax.ShapeDtypeStruct((COLS, 4, 128), F32),
        in_specs=[vmem, vmem],
        out_specs=vmem,
        scratch_shapes=[
            pltpu.VMEM((COLS, 8, 128), F32),
            pltpu.VMEM((8, ATOMS), F32),
            pltpu.VMEM((8, ATOMS), F32),
            pltpu.VMEM((128, ATOMS), BF16),
            pltpu.VMEM((OWN, 128), BF16),
            pltpu.VMEM((OWN, 128), BF16),
            pltpu.VMEM((OWN, ATOMS), BF16),
            pltpu.VMEM((16, ATOMS), BF16),
            pltpu.VMEM((OWN, 128), F32),
            pltpu.VMEM((1, HALF), F32),
            pltpu.VMEM((1, HALF), F32),
            pltpu.VMEM((1, HALF), F32),
            pltpu.VMEM((OWN, 128), F32),
            pltpu.VMEM((OWN, 128), F32),
            pltpu.VMEM((OWN, 128), jnp.int32),
            pltpu.VMEM((OWN, 128), F32),
            pltpu.VMEM((8, HALF), F32),
            pltpu.VMEM((16, HALF), F32),
            pltpu.VMEM((16, OWN), F32),
            pltpu.VMEM((1, HALF), F32),
            pltpu.VMEM((1, 4 * OWN), F32),
            pltpu.VMEM((4, ATOMS), F32),
            pltpu.VMEM((4, ATOMS), F32),
            pltpu.VMEM((8, 4, 128), F32),
            dma((COLS,)), dma((COLS,)),
            dma((ROWS,)), dma((ROWS,)),
            dma((ROWS,)), dma((ROWS,)),
            dma((ROWS,)), dma((ROWS,)),
            dma((ROWS,)), dma((ROWS,)),
            dma((COLS,)), dma((COLS,)),
        ],
        compiler_params=pltpu.CompilerParams(
            collective_id=0, has_side_effects=True, vmem_limit_bytes=56 * 2**20
        ),
    )(packed, exclusions[None, :])
    mine = lax.dynamic_slice_in_dim(result, (c % 4) * 32, 32, axis=2)
    return mine[:, 0:3], mine[:, 3]


def solution(mesh):
    return jax.shard_map(
        on_device,
        mesh=mesh,
        in_specs=(
            P(None, None, ("row", "col")),
            P(("row", "col")),
            P(("row", "col")),
            P("row"),
            P(),
            P(),
        ),
        out_specs=(P(None, None, ("row", "col")), P(None, ("row", "col"))),
        check_vma=False,
    )
```

```python
import functools
import math

import jax
import jax.numpy as jnp
from jax import lax
from jax.experimental import pallas as pl
from jax.experimental.pallas import tpu as pltpu
from jax.sharding import PartitionSpec as P

F32 = jnp.float32
BF16 = jnp.bfloat16
MESH = pl.DeviceIdType.MESH
TAU = 1.0 - 1.0 / 78.5
SIGMA = math.log2(math.e)
CENTRE = 32.0

ROWS = 8
COLS = 32
WIDE = 4
DEEP = 8
OWN = 1024
ATOMS = ROWS * OWN
HALF = 5 * OWN
STRIP = 256
CHUNK1 = 512
CHUNK2 = 512
PIECE = 64


def narrow(value):
    return value.astype(BF16).astype(F32)


def split3(value):
    first = narrow(value)
    second = narrow(value - first)
    return first, second, value - first - second


def row_index(shape):
    return lax.broadcasted_iota(jnp.int32, shape, 0)


def three_rows(value, at):
    pieces = split3(value)
    row = row_index((8, value.shape[1]))
    out = jnp.zeros((8, value.shape[1]), F32)
    for k, piece in enumerate(pieces):
        out = jnp.where(row == at + k, piece, out)
    return out


def features(block, left):
    n = block.shape[1]
    row = row_index((8, n))
    x = jnp.where(row < 3, block, 0.0)
    coarse = jnp.floor(x * 16.0 + 0.5) * 0.0625
    fine = x - coarse
    ch = narrow(coarse)
    cl = coarse - ch
    f1 = narrow(fine)
    f2 = narrow(fine - f1)
    norm = jnp.sum(coarse * coarse, axis=0, keepdims=True)
    rest = jnp.sum((2.0 * coarse + fine) * fine, axis=0, keepdims=True)
    ones_lo = jnp.where(row < 3, 1.0, 0.0)
    ones_mid = jnp.where((row >= 3) & (row < 6), 1.0, 0.0)
    if left:
        ch2, cl2, f12, f22 = (-2.0 * v for v in (ch, cl, f1, f2))
        groups = [ch2, ch2, cl2, cl2, three_rows(norm, 0) + ones_mid]
        groups += [ch2, ch2, cl2, cl2, f12, f12, f22, f22]
        groups += [f12 + three_rows(rest, 3), f12 + ones_mid, f22 + ones_mid]
    else:
        radius = block[4:5]
        groups = [ch, cl, ch, cl, ones_lo + three_rows(norm, 3)]
        groups += [f1, f2, f1, f2, ch, cl, ch, cl]
        groups += [f1 + ones_mid, f2 + three_rows(rest, 3), f1 + three_rows(radius * radius, 3)]
    return jnp.concatenate(groups, axis=0)


def weights(placed, scale):
    first, second, third = split3(placed * scale)
    return jnp.concatenate([first + pltpu.roll(second, 4, 0), third], axis=0).astype(BF16)


def gather_pieces(sums):
    top = sums[0:8]
    return top + pltpu.roll(top, 4, 0) + sums[8:16]


def spread(row, out_ref):
    for k in range(OWN // 128):
        piece = jnp.broadcast_to(row[:, k * 128 : (k + 1) * 128], (128, 128))
        out_ref[k * 128 : (k + 1) * 128, :] = jnp.transpose(piece)


def lane_sums(value):
    out = lax.dot_general(
        jnp.ones((8, 128), F32),
        value,
        (((1,), (1,)), ((), ())),
        precision=lax.Precision.HIGHEST,
        preferred_element_type=F32,
    )
    return out[0:1]


def run(steps):
    for _ in steps:
        pass


def weave(main, *others):
    side = [step for other in others for step in [other]]
    done = False
    turn = 0
    while True:
        if next(main, "end") == "end":
            break
        for other in side:
            next(other, None)
    for other in side:
        run(other)


def kernel(
    pos_ref, charge_ref, type_ref, excl_ref, radius_ref, volume_ref, force_ref, born_ref,
    padded, send, inbox, stage, outbox, final, atoms, placed, right, left, left2, cubes, weight, integral,
    born_all, damp_all, charge_row, damp_col, qborn_col, excl_col, rad_rows, rad_cols, side_cols,
    gaps, highs, lows,
    own_force, rad_send, rad_recv, force_send, force_recv, result,
    in_s, in_r, mid_s, mid_r, at_s, at_r, bn_s, bn_r, rd_s, rd_r, fc_s, fc_r, back_s, back_r, out_s, out_r,
):
    r = lax.axis_index("row")
    c = lax.axis_index("col")

    x = c // DEEP
    z = lax.rem(c, DEEP)

    def z_peer(d):
        return lax.rem(z + d, DEEP)

    def x_peer(d):
        return lax.rem(x + d, WIDE)

    def row_peer(d):
        return (lax.rem(r + d + ROWS, ROWS), c)

    barrier = pltpu.get_barrier_semaphore()
    for d in range(1, DEEP):
        pl.semaphore_signal(
            barrier, inc=1, device_id=(r, x * DEEP + z_peer(d)), device_id_type=MESH
        )
    for d in range(1, WIDE):
        pl.semaphore_signal(
            barrier, inc=1, device_id=(r, x_peer(d) * DEEP + z), device_id_type=MESH
        )
    for d in range(1, ROWS):
        pl.semaphore_signal(barrier, inc=1, device_id=row_peer(d), device_id_type=MESH)

    kinds = type_ref[...]
    radius = jnp.zeros((1, 32), F32)
    volume = jnp.zeros((1, 32), F32)
    for k in range(32):
        radius = jnp.where(kinds == k, radius_ref[k], radius)
        volume = jnp.where(kinds == k, volume_ref[k], volume)
    padded[...] = jnp.zeros_like(padded)
    for s in range(COLS):
        padded[s, 0:3, 0:32] = pos_ref[s]
        padded[s, 3:4, 0:32] = charge_ref[...]
        padded[s, 4:5, 0:32] = radius
        padded[s, 5:6, 0:32] = volume
    offset = lax.rem(c, 4) * 32
    for s in range(COLS):
        send[s % DEEP, s // DEEP] = pltpu.roll(padded[s], offset, 1)
    spread(excl_ref[...], excl_col)

    pl.semaphore_wait(barrier, DEEP - 1 + WIDE - 1 + ROWS - 1)

    def in_copy(d):
        return pltpu.make_async_remote_copy(
            src_ref=send.at[z_peer(d)], dst_ref=inbox.at[z],
            send_sem=in_s.at[d], recv_sem=in_r.at[d],
            device_id=(r, x * DEEP + z_peer(d)), device_id_type=MESH,
        )

    for d in range(1, DEEP):
        in_copy(d).start()
    inbox[z] = send[z]
    for d in range(1, DEEP):
        in_copy(d).wait_recv()
    for k in range(WIDE):
        for g in range(2):
            stage[k, :, g * 128 : (g + 1) * 128] = (inbox[4 * g, k] + inbox[4 * g + 1, k]) + (
                inbox[4 * g + 2, k] + inbox[4 * g + 3, k]
            )

    def mid_copy(d):
        return pltpu.make_async_remote_copy(
            src_ref=stage.at[x_peer(d)],
            dst_ref=atoms.at[:, pl.ds(pl.multiple_of(x * 256, 256), 256)],
            send_sem=mid_s.at[d], recv_sem=mid_r.at[d],
            device_id=(r, x_peer(d) * DEEP + z), device_id_type=MESH,
        )

    for d in range(1, WIDE):
        mid_copy(d).start()
    atoms[:, pl.ds(pl.multiple_of(x * 256, 256), 256)] = stage[x]
    for d in range(1, WIDE):
        mid_copy(d).wait_recv()

    def atom_copy(j):
        start = pl.multiple_of(j * OWN, OWN)
        return pltpu.make_async_remote_copy(
            src_ref=atoms.at[:, pl.ds(0, OWN)], dst_ref=atoms.at[:, pl.ds(start, OWN)],
            send_sem=at_s.at[j], recv_sem=at_r.at[j], device_id=row_peer(-j), device_id_type=MESH,
        )

    for j in range(1, ROWS):
        atom_copy(j).start()

    whole = features(atoms[:, 0:OWN], True)
    for k in range(OWN // 128):
        piece = jnp.transpose(whole[:, k * 128 : (k + 1) * 128])
        left[k * 128 : (k + 1) * 128, :] = piece.astype(BF16)
        lane = lax.broadcasted_iota(jnp.int32, (128, 128), 1)
        piece = jnp.where((lane >= 123) & (lane < 126), 0.0, piece)
        left2[k * 128 : (k + 1) * 128, :] = piece.astype(BF16)

    integral[...] = jnp.zeros_like(integral)

    def first_pass(j):
        base = pl.multiple_of(j * OWN, OWN)
        block = atoms[:, pl.ds(base, OWN)]
        right[:, pl.ds(base, OWN)] = features(block, False).astype(BF16)
        row = row_index((8, OWN))
        here = jnp.where(row < 3, block - CENTRE, jnp.where(row == 3, 1.0, 0.0))
        placed[:, pl.ds(base, OWN)] = here
        weight[:, pl.ds(base, OWN)] = weights(here, block[5:6])

        def near_dist(k):
            r0, c0, slot = (k % 4) * STRIP, (k // 4) * CHUNK1, k % 2
            for q in range(0, CHUNK1, 256):
                here = pl.ds(pl.multiple_of(base + c0 + q, 256), 256)
                gaps[slot, :, q : q + 256] = jnp.dot(
                    left[r0 : r0 + STRIP, :], right[:, here], preferred_element_type=F32
                )
                yield
                yield

        def near_terms(k):
            r0, c0, slot = (k % 4) * STRIP, (k // 4) * CHUNK1, k % 2
            for p in range(0, STRIP, PIECE):
                mine = slice(r0 + p, r0 + p + PIECE)
                total = None
                for q in range(0, CHUNK1, 128):
                    here = pl.ds(pl.multiple_of(base + c0 + q, 128), 128)
                    inverse = pl.reciprocal(gaps[slot, p : p + PIECE, q : q + 128], approx=True)
                    square = inverse * inverse
                    term = square * atoms[5:6, here]
                    total = term if total is None else total + term
                    cubes[mine, here] = (square * inverse).astype(BF16)
                    if q == CHUNK1 - 128:
                        integral[mine, :] += total
                    yield

        run(near_dist(0))
        for k in range(8):
            weave(near_terms(k), near_dist(k + 1) if k < 7 else iter(()))

    first_pass(0)

    @pl.loop(1, ROWS)
    def _(j):
        atom_copy(j).wait_recv()
        first_pass(j)

    charge = atoms[3:4, 0:OWN]
    radius = atoms[4:5, 0:OWN]
    volume = atoms[5:6, 0:OWN]
    own_inverse = 1.0 / (radius * radius)
    summed = lane_sums(integral[...]) - volume * own_inverse * own_inverse
    filled = jnp.tanh(radius * summed)
    born = 1.0 / (1.0 / radius - filled / (radius + 0.09))
    slope = born * born * (1.0 - filled * filled) * radius / (radius + 0.09)
    born_all[:, 0:OWN] = born

    def born_copy(j):
        return pltpu.make_async_remote_copy(
            src_ref=born_all.at[:, pl.ds(0, OWN)],
            dst_ref=born_all.at[:, pl.ds(pl.multiple_of(j * OWN, OWN), OWN)],
            send_sem=bn_s.at[j], recv_sem=bn_r.at[j], device_id=row_peer(-j), device_id_type=MESH,
        )

    for j in range(1, 5):
        born_copy(j).start()

    def own_descreen(j, sums):
        c0 = pl.multiple_of(j * OWN, OWN)
        return sums + lax.dot_general(
            weight[:, pl.ds(c0, OWN)], cubes[:, pl.ds(c0, OWN)],
            (((1,), (1,)), ((), ())), preferred_element_type=F32,
        )

    own_sums = lax.fori_loop(0, ROWS, own_descreen, jnp.zeros((16, OWN), F32))

    for j in range(1, 5):
        born_copy(j).wait_recv()

    radii = born_all[...]
    inverse_radii = 1.0 / radii
    damp = inverse_radii * (math.sqrt(SIGMA) * 0.5)
    damp_all[...] = damp
    lead = atoms[3:4, 0:HALF] * inverse_radii * lax.rsqrt(radii) * ((SIGMA * 0.25) ** 0.75)
    charge_row[...] = lead * radii
    weight[:, 0:HALF] = weights(placed[:, 0:HALF], lead)
    spread(damp[:, 0:OWN], damp_col)
    spread((lead * radii)[:, 0:OWN], qborn_col)
    rad_rows[...] = jnp.zeros_like(rad_rows)
    rad_cols[...] = jnp.zeros_like(rad_cols)
    side_cols[...] = jnp.zeros_like(side_cols)

    def dist(r0, rows, c0, cols, slot, at=0):
        wide = min(cols, 256)
        for q in range(0, cols, wide):
            here = pl.ds(pl.multiple_of(c0 + q, 128), wide)
            gaps[slot, at : at + rows, q : q + wide] = jnp.dot(
                left2[pl.ds(r0, rows), :], right[:, here], preferred_element_type=F32
            )
            yield

    def terms(r0, rows, c0, cols, special, both, slot, at=0):
        step = min(PIECE, rows)
        for q in range(cols // 128):
            here = pl.ds(pl.multiple_of(c0 + q * 128, 128), 128)
            lanes = slice(q * 128, (q + 1) * 128)
            damp_b = damp_all[:, here]
            charge_b = charge_row[:, here]
            total = None
            for p in range(0, rows, step):
                mine = pl.ds(pl.multiple_of(r0 + p, step), step)
                span = slice(at + p, at + p + step)
                y = gaps[slot, span, lanes] * (damp_col[mine, :] * damp_b)
                masked = special and abs(q * 128 - p) < max(step, 128) + 15
                if masked:
                    gap = (
                        lax.broadcasted_iota(jnp.int32, (step, 128), 1)
                        - lax.broadcasted_iota(jnp.int32, (step, 128), 0)
                        + (q * 128 - p)
                    )
                    near = jnp.abs(gap) <= 15
                    bit = jnp.where(gap > 0, gap - 1, 14 - gap)
                    bit = jnp.where(near & (gap != 0), bit, 0)
                    marked = jnp.bitwise_and(jnp.right_shift(excl_col[mine, :], bit), 1) == 1
                    drop = (near & marked) | (gap == 0)
                    y = jnp.where(gap == 0, 0.0, y)
                e = jnp.exp2(math.log2(SIGMA * 0.25) - y)
                g = lax.rsqrt(y + e)
                g3 = g * g * g
                i = lax.rsqrt(y)
                i3 = i * i * i
                if masked:
                    i3 = jnp.where(drop, 0.0, i3)
                h = g3 * e
                force = (i3 - TAU * g3) + (TAU / SIGMA) * h
                radial = h * (SIGMA + y)
                high = force.astype(BF16)
                highs[slot, span, lanes] = high
                lows[slot, span, lanes] = (force - high.astype(F32)).astype(BF16)
                rad_rows[mine, :] += radial * charge_b
                if q * 128 >= both:
                    part = radial * qborn_col[mine, :]
                    for k in range(step // 8):
                        piece = part[k * 8 : (k + 1) * 8]
                        total = piece if total is None else total + piece
                if p + step == rows and total is not None:
                    rad_cols[:, here] += total
                yield

    def sums(r0, rows, c0, cols, both, slot, at=0):
        wide = min(cols, 256)
        mine = weight[:, pl.ds(r0, rows)]
        for q in range(0, cols, wide):
            here = pl.ds(pl.multiple_of(c0 + q, 128), wide)
            there = weight[:, here]
            for store in (highs, lows):
                tile = store[slot, at : at + rows, q : q + wide]
                own_force[:, pl.ds(r0, rows)] += lax.dot_general(
                    there, tile, (((1,), (1,)), ((), ())), preferred_element_type=F32
                )
                yield
                if q >= both:
                    side_cols[:, here] += jnp.dot(mine, tile, preferred_element_type=F32)
                    yield

    own_force[...] = jnp.zeros_like(own_force)
    swap = jnp.where(r >= ROWS // 2, 128, 0)

    def tiles(s):
        r0 = pl.multiple_of(s * STRIP, STRIP)
        out = [[(r0, STRIP, r0, 2 * STRIP, True, STRIP, 0, 0)]]
        for t in range(7):
            c0 = pl.multiple_of(r0 + 2 * STRIP + t * CHUNK2, STRIP)
            out.append([(r0, STRIP, c0, CHUNK2, False, 0, (t + 1) % 2, 0)])
        far = r0 + 16 * STRIP
        out.append([
            (r0, 128, pl.multiple_of(far + swap, 128), 128, False, 0, 2, 0),
            (pl.multiple_of(r0 + 128, 128), 128, pl.multiple_of(far + 128 - swap, 128), 128, False, 0, 2, 128),
        ])
        return out

    def do_dist(group):
        for r0, rows, c0, cols, special, both, slot, at in group:
            yield from dist(r0, rows, c0, cols, slot, at)

    def do_sums(group):
        for r0, rows, c0, cols, special, both, slot, at in group:
            yield from sums(r0, rows, c0, cols, both, slot, at)

    def do_terms(group):
        for item in group:
            yield from terms(*item)

    strips = OWN // STRIP
    run(do_dist(tiles(0)[0]))
    highs[2] = jnp.zeros_like(highs[2])
    lows[2] = jnp.zeros_like(lows[2])

    @pl.loop(0, strips)
    def _(s):
        now = tiles(s)
        ahead = now[1:] + tiles(jnp.minimum(s + 1, strips - 1))[:1]
        behind = tiles(jnp.maximum(s - 1, 0))[-1:] + now[:-1]
        for group, later, earlier in zip(now, ahead, behind):
            weave(do_terms(group), do_sums(earlier), do_dist(later))

    run(do_sums(tiles(strips - 1)[-1]))

    rad_send[...] = jnp.sum(rad_cols[...], axis=0, keepdims=True)

    def rad_copy(j):
        return pltpu.make_async_remote_copy(
            src_ref=rad_send.at[:, pl.ds(j * OWN, OWN)],
            dst_ref=rad_recv.at[:, pl.ds((j - 1) * OWN, OWN)],
            send_sem=rd_s.at[j], recv_sem=rd_r.at[j], device_id=row_peer(j), device_id_type=MESH,
        )

    for j in range(1, 5):
        rad_copy(j).start()
    radial = lane_sums(rad_rows[...]) + rad_send[:, 0:OWN]
    for j in range(1, 5):
        rad_copy(j).wait_recv()
    for j in range(4):
        radial = radial + rad_recv[:, j * OWN : (j + 1) * OWN]
    lead_own = charge * lax.rsqrt(born) / born * ((SIGMA * 0.25) ** 0.75)
    radial = radial * lead_own * (0.5 * TAU * 4.0 / (SIGMA * SIGMA))
    chained = radial * slope
    chain_weight = weights(placed[:, 0:OWN], chained)

    def last_block(j, direct):
        c0 = pl.multiple_of(j * OWN, OWN)
        here = pl.ds(c0, OWN)
        sums = gather_pieces(jnp.dot(chain_weight, cubes[:, here], preferred_element_type=F32))
        where_b = placed[:, here]
        force = (where_b * sums[3:4] - sums) * (4.0 * atoms[5:6, here])
        if direct:
            side = gather_pieces(side_cols[:, here])
            damp_b = damp_all[:, here] * (2.0 / math.sqrt(SIGMA))
            lead_b = atoms[3:4, here] * damp_b * jnp.sqrt(damp_b) * ((SIGMA * 0.25) ** 0.75)
            force = force + (where_b * side[3:4] - side) * lead_b
        force_send[:, here] = force[0:4]

    def force_copy(j):
        here = pl.ds(pl.multiple_of(j * OWN, OWN), OWN)
        return pltpu.make_async_remote_copy(
            src_ref=force_send.at[:, here], dst_ref=force_recv.at[:, here],
            send_sem=fc_s.at[j], recv_sem=fc_r.at[j], device_id=row_peer(j), device_id_type=MESH,
        )

    @pl.loop(1, 5)
    def _(j):
        last_block(j, True)
        force_copy(j).start()

    @pl.loop(5, ROWS)
    def _(j):
        last_block(j, False)
        force_copy(j).start()

    last_block(0, True)
    mine = placed[:, 0:OWN]
    sums = gather_pieces(own_sums)
    total = (mine * sums[3:4] - sums) * (4.0 * chained)
    sums = gather_pieces(own_force[...])
    total = total + (mine * sums[3:4] - sums) * lead_own
    total = total[0:4] + force_send[:, 0:OWN]

    for j in range(1, ROWS):
        force_copy(j).wait_recv()
    for j in range(1, ROWS):
        total = total + force_recv[:, j * OWN : (j + 1) * OWN]
    total = jnp.where(row_index((4, OWN)) == 3, born, total)
    for g in range(OWN // 128):
        result[g] = total[:, g * 128 : (g + 1) * 128]

    def back_copy(d):
        return pltpu.make_async_remote_copy(
            src_ref=result.at[pl.ds(2 * x_peer(d), 2)], dst_ref=outbox.at[x],
            send_sem=back_s.at[d], recv_sem=back_r.at[d],
            device_id=(r, x_peer(d) * DEEP + z), device_id_type=MESH,
        )

    for d in range(1, WIDE):
        back_copy(d).start()
    outbox[x] = result[pl.ds(2 * x, 2)]
    for d in range(1, WIDE):
        back_copy(d).wait_recv()

    def out_copy(d):
        return pltpu.make_async_remote_copy(
            src_ref=outbox.at[:, z_peer(d) // 4], dst_ref=final.at[z],
            send_sem=out_s.at[d], recv_sem=out_r.at[d],
            device_id=(r, x * DEEP + z_peer(d)), device_id_type=MESH,
        )

    for d in range(1, DEEP):
        out_copy(d).start()
    final[z] = outbox[:, z // 4]
    for d in range(1, DEEP):
        out_copy(d).wait_recv()
    unroll = lax.rem(128 - offset, 128)
    for s in range(COLS):
        tile = pltpu.roll(final[s % DEEP, s // DEEP], unroll, 1)
        force_ref[s] = tile[0:3, 0:32]
        born_ref[s : s + 1, :] = tile[3:4, 0:32]

    for d in range(1, DEEP):
        in_copy(d).wait_send()
        out_copy(d).wait_send()
    for d in range(1, WIDE):
        mid_copy(d).wait_send()
        back_copy(d).wait_send()
    for j in range(1, 5):
        born_copy(j).wait_send()
        rad_copy(j).wait_send()
    for j in range(1, ROWS):
        atom_copy(j).wait_send()
        force_copy(j).wait_send()


def on_device(positions, charges, atom_types, exclusions, type_radius, type_volume):
    vmem = pl.BlockSpec(memory_space=pltpu.VMEM)
    dma = pltpu.SemaphoreType.DMA
    smem = pl.BlockSpec(memory_space=pltpu.SMEM)
    return pl.pallas_call(
        kernel,
        out_shape=[
            jax.ShapeDtypeStruct((COLS, 3, 32), F32),
            jax.ShapeDtypeStruct((COLS, 32), F32),
        ],
        in_specs=[vmem, vmem, vmem, vmem, smem, smem],
        out_specs=[vmem, vmem],
        scratch_shapes=[
            pltpu.VMEM((COLS, 8, 128), F32),
            pltpu.VMEM((DEEP, WIDE, 8, 128), F32),
            pltpu.VMEM((DEEP, WIDE, 8, 128), F32),
            pltpu.VMEM((WIDE, 8, 256), F32),
            pltpu.VMEM((WIDE, 2, 4, 128), F32),
            pltpu.VMEM((DEEP, WIDE, 4, 128), F32),
            pltpu.VMEM((8, ATOMS), F32),
            pltpu.VMEM((8, ATOMS), F32),
            pltpu.VMEM((128, ATOMS), BF16),
            pltpu.VMEM((OWN, 128), BF16),
            pltpu.VMEM((OWN, 128), BF16),
            pltpu.VMEM((OWN, ATOMS), BF16),
            pltpu.VMEM((16, ATOMS), BF16),
            pltpu.VMEM((OWN, 128), F32),
            pltpu.VMEM((1, HALF), F32),
            pltpu.VMEM((1, HALF), F32),
            pltpu.VMEM((1, HALF), F32),
            pltpu.VMEM((OWN, 128), F32),
            pltpu.VMEM((OWN, 128), F32),
            pltpu.VMEM((OWN, 128), jnp.int32),
            pltpu.VMEM((OWN, 128), F32),
            pltpu.VMEM((8, HALF), F32),
            pltpu.VMEM((16, HALF), F32),
            pltpu.VMEM((3, STRIP, CHUNK2), F32),
            pltpu.VMEM((3, STRIP, CHUNK2), BF16),
            pltpu.VMEM((3, STRIP, CHUNK2), BF16),
            pltpu.VMEM((16, OWN), F32),
            pltpu.VMEM((1, HALF), F32),
            pltpu.VMEM((1, 4 * OWN), F32),
            pltpu.VMEM((4, ATOMS), F32),
            pltpu.VMEM((4, ATOMS), F32),
            pltpu.VMEM((8, 4, 128), F32),
            dma((DEEP,)), dma((DEEP,)),
            dma((WIDE,)), dma((WIDE,)),
            dma((ROWS,)), dma((ROWS,)),
            dma((ROWS,)), dma((ROWS,)),
            dma((ROWS,)), dma((ROWS,)),
            dma((ROWS,)), dma((ROWS,)),
            dma((WIDE,)), dma((WIDE,)),
            dma((DEEP,)), dma((DEEP,)),
        ],
        compiler_params=pltpu.CompilerParams(
            collective_id=0, has_side_effects=True, vmem_limit_bytes=56 * 2**20
        ),
    )(
        positions, charges[None, :], atom_types[None, :], exclusions[None, :],
        type_radius, type_volume,
    )


def solution(mesh):
    return jax.shard_map(
        on_device,
        mesh=mesh,
        in_specs=(
            P(None, None, ("row", "col")),
            P(("row", "col")),
            P(("row", "col")),
            P("row"),
            P(),
            P(),
        ),
        out_specs=(P(None, None, ("row", "col")), P(None, ("row", "col"))),
        check_vma=False,
    )
```

```python
import math

import jax
import jax.numpy as jnp
from jax import lax
from jax.experimental import pallas as pl
from jax.experimental.pallas import tpu as pltpu
from jax.sharding import PartitionSpec as P

F32 = jnp.float32
BF16 = jnp.bfloat16
MESH = pl.DeviceIdType.MESH
TAU = 1.0 - 1.0 / 78.5
SIGMA = math.log2(math.e)
CENTRE = 32.0
GRID = 1.5 * 2.0**19

ROWS = 8
COLS = 32
OWN = 1024
ATOMS = ROWS * OWN
HALF = 5 * OWN
STRIP = 256
CHUNK1 = 512
CHUNK2 = 512
PIECE = 64


def narrow(value):
    return value.astype(BF16).astype(F32)


def split3(value):
    first = narrow(value)
    second = narrow(value - first)
    return first, second, value - first - second


def row_index(shape):
    return lax.broadcasted_iota(jnp.int32, shape, 0)


def at_rows(shape, *pairs):
    row = row_index(shape)
    out = jnp.zeros(shape, F32)
    for k, value in pairs:
        out = jnp.where(row == k, value, out)
    return out


def features(block, left):
    shape = block.shape
    row = row_index(shape)
    first = row < 3
    x = jnp.where(first, block, 0.0)
    x = x + pltpu.roll(x, 4, 0)
    coarse = (x + GRID) - GRID
    fine = x - coarse
    ch = narrow(coarse)
    cl = coarse - ch
    f1 = narrow(fine)
    f2 = fine - f1
    norm = jnp.sum(jnp.where(first, coarse * coarse, 0.0), axis=0, keepdims=True)
    rest = jnp.sum(jnp.where(first, (2.0 * coarse + fine) * fine, 0.0), axis=0, keepdims=True)
    empty = jnp.zeros(shape, F32)
    if left:
        n1, n2, n3 = split3(norm)
        r1, r2, r3 = split3(rest)
        ch, cl, f1, f2 = (-2.0 * v for v in (ch, cl, f1, f2))
        groups = [ch, cl]
        ones = jnp.where(row < 3, 1.0, 0.0)
        groups += [ones + at_rows(shape, (3, n1), (4, n2), (5, n3)), ch, cl, f1, f2, f1]
        groups += [jnp.where(row < 4, f2, 0.0), ones + at_rows(shape, (3, r1), (4, r2), (5, r3)), ones]
    else:
        grid = jnp.where(row < 4, ch, cl)
        tail = jnp.where(row < 4, f1, f2)
        n1, n2, n3 = split3(norm)
        r1, r2, r3 = split3(rest)
        s1, s2, s3 = split3(block[4:5] * block[4:5])
        ones = jnp.where((row > 2) & (row < 6), 1.0, 0.0)
        exact = ones + at_rows(shape, (0, n1), (1, n2), (2, n3))
        small = ones + at_rows(shape, (0, r1), (1, r2), (2, r3))
        own = at_rows(shape, (0, s1), (1, s2), (2, s3))
        groups = [grid, grid, exact, tail, tail, grid, grid, tail, tail, small, own]
    return jnp.concatenate(groups + [empty] * (16 - len(groups)), axis=0)


def weights(placed, scale, extra=None):
    first, second, third = split3(placed * scale)
    if extra is not None:
        for k, piece in enumerate(split3(extra)):
            third = jnp.where(row_index(third.shape) == 4 + k, piece, third)
    return jnp.concatenate([first + pltpu.roll(second, 4, 0), third], axis=0).astype(BF16)


def gather_pieces(sums):
    top = sums[0:8]
    return top + pltpu.roll(top, 4, 0) + sums[8:16]


def spread(row, out_ref):
    for k in range(OWN // 128):
        piece = jnp.broadcast_to(row[:, k * 128 : (k + 1) * 128], (128, 128))
        out_ref[k * 128 : (k + 1) * 128, :] = jnp.transpose(piece)


def lane_sums(value):
    out = lax.dot_general(
        jnp.ones((8, 128), F32),
        value,
        (((1,), (1,)), ((), ())),
        precision=lax.Precision.HIGHEST,
        preferred_element_type=F32,
    )
    return out[0:1]


def run(steps):
    for _ in steps:
        pass


def weave(main, *others):
    side = [step for other in others for step in [other]]
    done = False
    turn = 0
    while True:
        if next(main, "end") == "end":
            break
        for other in side:
            next(other, None)
    for other in side:
        run(other)


def kernel(
    pos_ref, charge_ref, type_ref, excl_ref, radius_ref, volume_ref, force_ref, born_ref,
    send, inbox, final, atoms, placed, right, left, left2, cubes, weight, weight2, integral,
    born_all, damp_all, charge_row, damp_col, excl_col, rad_rows, side_rad, side_cols, own_sums,
    gaps, highs, lows, rads,
    own_force, rad_send, rad_recv, force_send, force_recv, result,
    in_s, in_r, at_s, at_r, bn_s, bn_r, rd_s, rd_r, fc_s, fc_r, out_s, out_r,
):
    r = lax.axis_index("row")
    c = lax.axis_index("col")

    def row_peer(d):
        return (lax.rem(r + d + ROWS, ROWS), c)

    def col_peer(d):
        return (r, lax.rem(c + d, COLS))

    barrier = pltpu.get_barrier_semaphore()
    for d in range(1, COLS):
        pl.semaphore_signal(barrier, inc=1, device_id=col_peer(d), device_id_type=MESH)
    for d in range(1, ROWS):
        pl.semaphore_signal(barrier, inc=1, device_id=row_peer(d), device_id_type=MESH)

    kinds = type_ref[...]
    radius = jnp.zeros((1, 32), F32)
    volume = jnp.zeros((1, 32), F32)
    for k in range(32):
        radius = jnp.where(kinds == k, radius_ref[k], radius)
        volume = jnp.where(kinds == k, volume_ref[k], volume)
    fields = [pos_ref[0], pos_ref[1], pos_ref[2]]
    fields += [jnp.broadcast_to(v, (COLS, 32)) for v in (charge_ref[...], radius, volume)]
    fields += [jnp.zeros((COLS, 32), F32)] * 2
    packed = jnp.concatenate(fields, axis=1)
    for s in range(COLS):
        send[s] = packed[s : s + 1, :]
    spread(excl_ref[...], excl_col)

    pl.semaphore_wait(barrier, COLS - 1 + ROWS - 1)

    def in_copy(d):
        peer = col_peer(d)
        return pltpu.make_async_remote_copy(
            src_ref=send.at[peer[1]], dst_ref=inbox.at[c],
            send_sem=in_s.at[d], recv_sem=in_r.at[d], device_id=peer, device_id_type=MESH,
        )

    for d in range(1, COLS):
        in_copy(d).start()
    inbox[c] = send[c]
    for d in range(1, COLS):
        in_copy(d).wait_recv()
    sub = row_index((8, 128))
    quarter = lax.broadcasted_iota(jnp.int32, (8, 128), 1) // 32
    for g in range(OWN // 128):
        tile = jnp.zeros((8, 128), F32)
        for k in range(4):
            row = inbox[4 * g + k]
            both = jnp.where(
                sub < 4,
                jnp.broadcast_to(row[:, 0:128], (8, 128)),
                jnp.broadcast_to(row[:, 128:256], (8, 128)),
            )
            both = jnp.where(jnp.bitwise_and(sub, 1) == 1, pltpu.roll(both, 96, 1), both)
            both = jnp.where(jnp.bitwise_and(sub, 2) == 2, pltpu.roll(both, 64, 1), both)
            if k:
                both = pltpu.roll(both, 32 * k, 1)
            tile = jnp.where(quarter == k, both, tile)
        atoms[:, g * 128 : (g + 1) * 128] = jnp.where(sub < 6, tile, 0.0)

    def atom_copy(j):
        start = pl.multiple_of(j * OWN, OWN)
        return pltpu.make_async_remote_copy(
            src_ref=atoms.at[0:6, pl.ds(0, OWN)], dst_ref=atoms.at[0:6, pl.ds(start, OWN)],
            send_sem=at_s.at[j], recv_sem=at_r.at[j], device_id=row_peer(-j), device_id_type=MESH,
        )

    y = r // 2

    def slot_of(t):
        k = t // 2
        turn = lax.rem(y + k + k // 2 - 2 * (k // 3), 4)
        core = lax.rem(r + t, 2)
        return lax.rem(turn * 2 + core - r + ROWS, ROWS)

    for t in range(1, ROWS):
        atom_copy(slot_of(ROWS - t)).start()

    whole = features(atoms[:, 0:OWN], True)
    for k in range(OWN // 128):
        piece = jnp.transpose(whole[:, k * 128 : (k + 1) * 128])
        left[k * 128 : (k + 1) * 128, :] = piece.astype(BF16)
        lane = lax.broadcasted_iota(jnp.int32, (128, 128), 1)
        piece = jnp.where((lane >= 80) & (lane < 88), 0.0, piece)
        left2[k * 128 : (k + 1) * 128, :] = piece.astype(BF16)

    integral[...] = jnp.zeros_like(integral)

    def first_pass(j):
        base = pl.multiple_of(j * OWN, OWN)
        block = atoms[:, pl.ds(base, OWN)]
        right[:, pl.ds(base, OWN)] = features(block, False).astype(BF16)
        row = row_index((8, OWN))
        here = jnp.where(row < 3, block - CENTRE, jnp.where(row == 3, 1.0, 0.0))
        placed[:, pl.ds(base, OWN)] = here
        weight[:, pl.ds(base, OWN)] = weights(here, block[5:6])

        def near_dist(k):
            r0, c0, slot = (k % 4) * STRIP, (k // 4) * CHUNK1, k % 2
            for q in range(0, CHUNK1, 256):
                here = pl.ds(pl.multiple_of(base + c0 + q, 256), 256)
                gaps[slot, :, q : q + 256] = jnp.dot(
                    left[r0 : r0 + STRIP, :], right[:, here], preferred_element_type=F32
                )
                yield
                yield

        def near_terms(k):
            r0, c0, slot = (k % 4) * STRIP, (k // 4) * CHUNK1, k % 2
            for p in range(0, STRIP, PIECE):
                mine = slice(r0 + p, r0 + p + PIECE)
                total = None
                for q in range(0, CHUNK1, 128):
                    here = pl.ds(pl.multiple_of(base + c0 + q, 128), 128)
                    inverse = pl.reciprocal(gaps[slot, p : p + PIECE, q : q + 128], approx=True)
                    square = inverse * inverse
                    term = square * atoms[5:6, here]
                    total = term if total is None else total + term
                    cubes[mine, here] = (square * inverse).astype(BF16)
                    if q == CHUNK1 - 128:
                        integral[mine, :] += total
                    yield

        run(near_dist(0))
        for k in range(8):
            weave(near_terms(k), near_dist(k + 1) if k < 7 else iter(()))

    first_pass(0)

    @pl.loop(1, ROWS)
    def _(t):
        j = slot_of(t)
        atom_copy(j).wait_recv()
        first_pass(j)

    charge = atoms[3:4, 0:OWN]
    radius = atoms[4:5, 0:OWN]
    volume = atoms[5:6, 0:OWN]
    own_inverse = 1.0 / (radius * radius)
    summed = lane_sums(integral[...]) - volume * own_inverse * own_inverse
    filled = jnp.tanh(radius * summed)
    born = 1.0 / (1.0 / radius - filled / (radius + 0.09))
    slope = born * born * (1.0 - filled * filled) * radius / (radius + 0.09)
    born_all[:, 0:OWN] = born

    def born_copy(j):
        return pltpu.make_async_remote_copy(
            src_ref=born_all.at[:, pl.ds(0, OWN)],
            dst_ref=born_all.at[:, pl.ds(pl.multiple_of(j * OWN, OWN), OWN)],
            send_sem=bn_s.at[j], recv_sem=bn_r.at[j], device_id=row_peer(-j), device_id_type=MESH,
        )

    for j in range(1, 5):
        born_copy(j).start()

    rad_rows[...] = jnp.zeros_like(rad_rows)
    side_rad[...] = jnp.zeros_like(side_rad)
    side_cols[...] = jnp.zeros_like(side_cols)
    own_sums[...] = jnp.zeros_like(own_sums)

    def prepare(j):
        here = pl.ds(pl.multiple_of(j * OWN, OWN), OWN)
        radii = born_all[:, here]
        inverse_radii = 1.0 / radii
        damp = inverse_radii * (math.sqrt(SIGMA) * 0.5)
        damp_all[:, here] = damp
        lead = atoms[3:4, here] * inverse_radii * lax.rsqrt(radii) * ((SIGMA * 0.25) ** 0.75)
        charge_row[:, here] = lead * radii
        weight2[:, here] = weights(placed[:, here], lead, lead * radii)
        return damp, lead * radii

    damp, qborn = prepare(0)
    spread(damp, damp_col)

    def dist(r0, rows, c0, cols, slot, at=0):
        wide = min(cols, 256)
        for q in range(0, cols, wide):
            here = pl.ds(pl.multiple_of(c0 + q, 128), wide)
            gaps[slot, at : at + rows, q : q + wide] = jnp.dot(
                left2[pl.ds(r0, rows), :], right[:, here], preferred_element_type=F32
            )
            yield

    def terms(r0, rows, c0, cols, special, both, slot, at=0):
        step = min(PIECE, rows)
        skew = c0 - r0
        for q in range(cols // 128):
            here = pl.ds(pl.multiple_of(c0 + q * 128, 128), 128)
            lanes = slice(q * 128, (q + 1) * 128)
            damp_b = damp_all[:, here]
            for p in range(0, rows, step):
                mine = pl.ds(pl.multiple_of(r0 + p, step), step)
                span = slice(at + p, at + p + step)
                y = gaps[slot, span, lanes] * (damp_col[mine, :] * damp_b)
                masked = special is not None and -143 < special + q * 128 - p < step + 15
                if masked:
                    gap = (
                        lax.broadcasted_iota(jnp.int32, (step, 128), 1)
                        - lax.broadcasted_iota(jnp.int32, (step, 128), 0)
                        + (q * 128 - p + skew)
                    )
                    near = jnp.abs(gap) <= 15
                    bit = jnp.where(gap > 0, gap - 1, 14 - gap)
                    bit = jnp.where(near & (gap != 0), bit, 0)
                    marked = jnp.bitwise_and(jnp.right_shift(excl_col[mine, :], bit), 1) == 1
                    drop = (near & marked) | (gap == 0)
                    y = jnp.where(gap == 0, 0.0, y)
                e = jnp.exp2(math.log2(SIGMA * 0.25) - y)
                g = lax.rsqrt(y + e)
                g3 = g * g * g
                i = lax.rsqrt(y)
                i3 = i * i * i
                if masked:
                    i3 = jnp.where(drop, 0.0, i3)
                h = g3 * e
                force = (i3 - TAU * g3) + (TAU / SIGMA) * h
                radial = h * (SIGMA + y)
                high = force.astype(BF16)
                highs[slot, span, lanes] = high
                lows[slot, span, lanes] = (force - high.astype(F32)).astype(BF16)
                rad_rows[mine, :] += radial * charge_row[:, here]
                rads[slot, span, lanes] = radial.astype(BF16)
                yield

    def sums(r0, rows, c0, cols, both, slot, at=0):
        wide = min(cols, 256)
        mine = weight2[:, pl.ds(r0, rows)]
        for q in range(0, cols, wide):
            here = pl.ds(pl.multiple_of(c0 + q, 128), wide)
            there = weight2[:, here]
            for store in (highs, lows):
                tile = store[slot, at : at + rows, q : q + wide]
                own_force[:, pl.ds(r0, rows)] += lax.dot_general(
                    there, tile, (((1,), (1,)), ((), ())), preferred_element_type=F32
                )
                yield
                if q >= both:
                    side_cols[:, here] += jnp.dot(mine, tile, preferred_element_type=F32)
                    yield
            if q >= both:
                tile = rads[slot, at : at + rows, q : q + wide]
                side_rad[:, here] += jnp.dot(mine, tile, preferred_element_type=F32)
                yield

    own_force[...] = jnp.zeros_like(own_force)
    swap = jnp.where(r >= ROWS // 2, 128, 0)

    def do_dist(group):
        for r0, rows, c0, cols, special, both, slot, at in group:
            yield from dist(r0, rows, c0, cols, slot, at)

    def do_sums(group):
        for r0, rows, c0, cols, special, both, slot, at in group:
            yield from sums(r0, rows, c0, cols, both, slot, at)

    def do_terms(group):
        for item in group:
            yield from terms(*item)

    def drive(groups, before, after):
        for k, group in enumerate(groups):
            earlier = groups[k - 1] if k else before
            later = groups[k + 1] if k + 1 < len(groups) else after
            weave(do_terms(group), do_sums(earlier), do_dist(later))

    def own_descreen(j):
        for q in range(0, OWN, 256):
            here = pl.ds(pl.multiple_of(j * OWN + q, 256), 256)
            for p in range(0, OWN, STRIP):
                own_sums[:, p : p + STRIP] += lax.dot_general(
                    weight[:, here], cubes[p : p + STRIP, here], (((1,), (1,)), ((), ())),
                    preferred_element_type=F32,
                )
                yield

    def column_block(j):
        base = pl.multiple_of(j * OWN, OWN)
        groups = []
        for k in range(8):
            r0, c0 = (k // 2) * STRIP, base + (k % 2) * CHUNK2
            special = 256 if k == 6 else None
            groups.append([(r0, STRIP, pl.multiple_of(c0, CHUNK2), CHUNK2, special, 0, k % 2, 0)])
        return groups

    near = [
        [(0, 256, 0, 512, 0, 256, 0, 0)],
        [(0, 256, 512, 512, None, 0, 1, 0)],
        [(256, 256, 256, 512, 0, 256, 0, 0)],
        [(256, 256, 768, 256, None, 0, 1, 0)],
        [(512, 256, 512, 512, 0, 256, 0, 0)],
        [(768, 256, 768, 256, 0, 256, 1, 0)],
    ]
    run(do_dist(near[0]))
    drive(near, [], column_block(1)[0])
    run(do_sums(near[-1]))
    highs[1] = jnp.zeros_like(highs[1])
    lows[1] = jnp.zeros_like(lows[1])
    rads[1] = jnp.zeros_like(rads[1])

    def rad_copy(j):
        return pltpu.make_async_remote_copy(
            src_ref=rad_send.at[:, pl.ds(pl.multiple_of(j * OWN, OWN), OWN)],
            dst_ref=rad_recv.at[:, pl.ds(pl.multiple_of((j - 1) * OWN, OWN), OWN)],
            send_sem=rd_s.at[j], recv_sem=rd_r.at[j], device_id=row_peer(j), device_id_type=MESH,
        )

    def send_radial(j):
        here = pl.ds(pl.multiple_of(j * OWN, OWN), OWN)
        rad_send[:, here] = jnp.sum(side_rad[12:15, here], axis=0, keepdims=True)
        rad_copy(j).start()

    @pl.loop(1, 4)
    def _(j):
        born_copy(j).wait_recv()
        prepare(j)
        drive(column_block(j), column_block(j - 1)[-1], column_block(j + 1)[0])

        @pl.when(j > 1)
        def _():
            send_radial(j - 1)

    run(do_sums(column_block(3)[-1]))
    send_radial(3)
    born_copy(4).wait_recv()
    prepare(4)
    base = 4 * OWN
    far = [
        [(256, 256, base, 256, None, 0, 0, 0)],
        [(512, 256, base, 512, None, 0, 1, 0)],
        [(768, 256, base, 512, None, 0, 0, 0)],
        [(768, 256, base + 512, 256, None, 0, 1, 0)],
    ]
    for k in range(4):
        r0, c0 = k * STRIP, base + k * STRIP
        far.append([
            (r0, 128, pl.multiple_of(c0 + swap, 128), 128, None, 0, k % 2, 0),
            (r0 + 128, 128, pl.multiple_of(c0 + 128 - swap, 128), 128, None, 0, k % 2, 128),
        ])
    run(do_dist(far[0]))
    drive(far, [], [])
    run(do_sums(far[-1]))
    send_radial(4)

    @pl.loop(0, 5)
    def _(j):
        run(own_descreen(j))

    radial = jnp.sum(side_rad[12:15, 0:OWN], axis=0, keepdims=True) + lane_sums(rad_rows[...])
    for j in range(1, 5):
        rad_copy(j).wait_recv()
    for j in range(4):
        radial = radial + rad_recv[:, j * OWN : (j + 1) * OWN]
    lead_own = charge * lax.rsqrt(born) / born * ((SIGMA * 0.25) ** 0.75)
    radial = radial * lead_own * (0.5 * TAU * 4.0 / (SIGMA * SIGMA))
    chained = radial * slope
    chain_weight = weights(placed[:, 0:OWN], chained)

    def last_block(j, direct):
        c0 = pl.multiple_of(j * OWN, OWN)
        here = pl.ds(c0, OWN)
        sums = gather_pieces(jnp.dot(chain_weight, cubes[:, here], preferred_element_type=F32))
        where_b = placed[:, here]
        force = (where_b * sums[3:4] - sums) * (4.0 * atoms[5:6, here])
        if direct:
            side = gather_pieces(side_cols[:, here])
            damp_b = damp_all[:, here] * (2.0 / math.sqrt(SIGMA))
            lead_b = atoms[3:4, here] * damp_b * jnp.sqrt(damp_b) * ((SIGMA * 0.25) ** 0.75)
            force = force + (where_b * side[3:4] - side) * lead_b
        force_send[:, here] = force[0:4]

    def force_copy(j):
        here = pl.ds(pl.multiple_of(j * OWN, OWN), OWN)
        return pltpu.make_async_remote_copy(
            src_ref=force_send.at[:, here], dst_ref=force_recv.at[:, here],
            send_sem=fc_s.at[j], recv_sem=fc_r.at[j], device_id=row_peer(j), device_id_type=MESH,
        )

    @pl.loop(1, 5)
    def _(j):
        last_block(j, True)
        force_copy(j).start()

    @pl.loop(5, ROWS)
    def _(j):
        last_block(j, False)
        force_copy(j).start()

    last_block(0, True)

    @pl.loop(5, ROWS)
    def _(j):
        run(own_descreen(j))

    mine = placed[:, 0:OWN]
    sums = gather_pieces(own_sums[...])
    total = (mine * sums[3:4] - sums) * (4.0 * chained)
    sums = gather_pieces(own_force[...])
    total = total + (mine * sums[3:4] - sums) * lead_own
    total = total[0:4] + force_send[:, 0:OWN]

    for j in range(1, ROWS):
        force_copy(j).wait_recv()
    for j in range(1, ROWS):
        total = total + force_recv[:, j * OWN : (j + 1) * OWN]
    total = jnp.where(row_index((4, OWN)) == 3, born, total)
    for g in range(OWN // 128):
        result[g] = total[:, g * 128 : (g + 1) * 128]

    def out_copy(d):
        peer = col_peer(d)
        return pltpu.make_async_remote_copy(
            src_ref=result.at[peer[1] // 4], dst_ref=final.at[c],
            send_sem=out_s.at[d], recv_sem=out_r.at[d], device_id=peer, device_id_type=MESH,
        )

    for d in range(1, COLS):
        out_copy(d).start()
    final[c] = result[c // 4]
    for d in range(1, COLS):
        out_copy(d).wait_recv()
    unroll = lax.rem(128 - lax.rem(c, 4) * 32, 128)
    for s in range(COLS):
        tile = pltpu.roll(final[s], unroll, 1)
        for f in range(3):
            force_ref[f, s : s + 1, :] = tile[f : f + 1, 0:32]
        born_ref[s : s + 1, :] = tile[3:4, 0:32]

    for d in range(1, COLS):
        in_copy(d).wait_send()
        out_copy(d).wait_send()
    for j in range(1, 5):
        born_copy(j).wait_send()
        rad_copy(j).wait_send()
    for j in range(1, ROWS):
        atom_copy(j).wait_send()
        force_copy(j).wait_send()


def on_device(positions, charges, atom_types, exclusions, type_radius, type_volume):
    vmem = pl.BlockSpec(memory_space=pltpu.VMEM)
    dma = pltpu.SemaphoreType.DMA
    smem = pl.BlockSpec(memory_space=pltpu.SMEM)
    forces, born = pl.pallas_call(
        kernel,
        out_shape=[
            jax.ShapeDtypeStruct((3, COLS, 32), F32),
            jax.ShapeDtypeStruct((COLS, 32), F32),
        ],
        in_specs=[vmem, vmem, vmem, vmem, smem, smem],
        out_specs=[vmem, vmem],
        scratch_shapes=[
            pltpu.VMEM((COLS, 1, 256), F32),
            pltpu.VMEM((COLS, 1, 256), F32),
            pltpu.VMEM((COLS, 4, 128), F32),
            pltpu.VMEM((8, ATOMS), F32),
            pltpu.VMEM((8, ATOMS), F32),
            pltpu.VMEM((128, ATOMS), BF16),
            pltpu.VMEM((OWN, 128), BF16),
            pltpu.VMEM((OWN, 128), BF16),
            pltpu.VMEM((OWN, ATOMS), BF16),
            pltpu.VMEM((16, ATOMS), BF16),
            pltpu.VMEM((16, HALF), BF16),
            pltpu.VMEM((OWN, 128), F32),
            pltpu.VMEM((1, HALF), F32),
            pltpu.VMEM((1, HALF), F32),
            pltpu.VMEM((1, HALF), F32),
            pltpu.VMEM((OWN, 128), F32),
            pltpu.VMEM((OWN, 128), jnp.int32),
            pltpu.VMEM((OWN, 128), F32),
            pltpu.VMEM((16, HALF), F32),
            pltpu.VMEM((16, HALF), F32),
            pltpu.VMEM((16, OWN), F32),
            pltpu.VMEM((2, STRIP, CHUNK2), F32),
            pltpu.VMEM((2, STRIP, CHUNK2), BF16),
            pltpu.VMEM((2, STRIP, CHUNK2), BF16),
            pltpu.VMEM((2, STRIP, CHUNK2), BF16),
            pltpu.VMEM((16, OWN), F32),
            pltpu.VMEM((1, HALF), F32),
            pltpu.VMEM((1, 4 * OWN), F32),
            pltpu.VMEM((4, ATOMS), F32),
            pltpu.VMEM((4, ATOMS), F32),
            pltpu.VMEM((8, 4, 128), F32),
            dma((COLS,)), dma((COLS,)),
            dma((ROWS,)), dma((ROWS,)),
            dma((ROWS,)), dma((ROWS,)),
            dma((ROWS,)), dma((ROWS,)),
            dma((ROWS,)), dma((ROWS,)),
            dma((COLS,)), dma((COLS,)),
        ],
        compiler_params=pltpu.CompilerParams(
            collective_id=0, has_side_effects=True, vmem_limit_bytes=56 * 2**20
        ),
    )(
        positions.transpose(1, 0, 2), charges[None, :], atom_types[None, :], exclusions[None, :],
        type_radius, type_volume,
    )
    return forces.transpose(1, 0, 2), born


def solution(mesh):
    return jax.shard_map(
        on_device,
        mesh=mesh,
        in_specs=(
            P(None, None, ("row", "col")),
            P(("row", "col")),
            P(("row", "col")),
            P("row"),
            P(),
            P(),
        ),
        out_specs=(P(None, None, ("row", "col")), P(None, ("row", "col"))),
        check_vma=False,
    )
```
